256 devices in a mesh: island: 16 (over x, y_hi, core), expert: 16 (over z, y_lo).
Axes of the slice: x: 4, y: 4 (y_hi: 2, y_lo: 2; y = y_hi * 2 + y_lo), z: 8, core: 2. Of those that a mesh axis runs over, the one named last changes fastest.
Arguments:
- tokens: bfloat16 [16, 1, 2048, 2048], P('island', None, 'expert'), may hold values from -6 to 6
- targets: bfloat16 [16, 1, 2048, 2048], P('island', None, 'expert'), may hold values from -3 to 3
- expert_ids: int32 [16, 1, 2048, 8], P('island', None, 'expert'), may hold values from 0 to 15, all different within a row; in each aligned block of 128 rows (0 to 127, 128 to 255, ..., all dimensions but the last counted through in order) at most 80 rows name the same one
- route_weight: float32 [16, 1, 2048, 8], P('island', None, 'expert'), may hold values from 0.05 to 1
- w_gate: bfloat16 [16, 16, 2048, 384], P('island', 'expert'), may hold values from -5 to 5
- w_up: bfloat16 [16, 16, 2048, 384], P('island', 'expert'), may hold values from -5 to 5
- w_down: bfloat16 [16, 16, 384, 2048], P('island', 'expert'), may hold values from -5 to 5
- prev_delta: bfloat16 [16, 16, 384, 2048], P('island', 'expert'), may hold values from -2 to 2
- global_params: float32 [16, 384, 2048], P('expert', 'island'), may hold values from -5 to 5
- momentum: float32 [16, 384, 2048], P('expert', 'island'), may hold values from -2 to 2
Outputs:
- new_gate: bfloat16 [16, 16, 2048, 384], P('island', 'expert')
- new_up: bfloat16 [16, 16, 2048, 384], P('island', 'expert')
- new_down: bfloat16 [16, 16, 384, 2048], P('island', 'expert')
- new_global: float32 [16, 384, 2048], P('expert', 'island')
- new_momentum: float32 [16, 384, 2048], P('expert', 'island')
The draws below stay inside these ranges and needn't reach their ends.
Inputs may be any that keep to these rules, and one draw needn't show every extreme that they name: `expert_ids`: each token names 8 different experts; among the 128 tokens of one device in one inner step, at most 80 name the same expert.
All inputs are finite; a program needn't handle non-finite values.
Results may differ from the reference program's by a relative error of at most 0.02.
Values may be sent and summed in bfloat16 or wider, within the bound.
No kernel may reach another device: no remote copies, remote signals or barrier semaphores. Data moves between devices by JAX's collectives and lax.ppermute only.
A program may use at most 128 MiB of HBM per device.

```python
import math
import jax
import jax.numpy as jnp
import numpy as np
from jax import lax

D = 2048
HID = 384
STEPS = 1
TOK_DEV = 128
EXPERTS = 16
TOP = 8
CAP = 80
ISL_TOK = 2048
ISLANDS = 16
N_EXPERT = 16


def with_spikes(values, own_key, source, target, shards_of, factor):
    def block_of(axis_at):
        return (jnp.arange(values.shape[axis_at]) // (values.shape[axis_at] // shards_of)).reshape((-1,) + (1,) * (values.ndim - 1 - axis_at))

    one_side = jax.random.permutation(own_key, shards_of)[block_of(target)]
    other_side = (block_of(target) + shards_of // 2) % shards_of
    return jnp.where((block_of(source) == one_side) | (block_of(source) == other_side), factor * values, values)


def steps_of(rng, shape, shards, smallest, top_value):
    def one(dim, shards_of):
        steps = jax.random.uniform(jax.random.fold_in(jax.random.fold_in(rng, 6), dim), (shards_of,), jnp.float32, smallest / len(shards), top_value / len(shards))
        return jnp.repeat(jnp.exp(steps), shape[dim] // shards_of).reshape((-1,) + (1,) * (len(shape) - dim - 1))

    factor_of = one(*shards[0])
    for cut in shards[1:]:
        factor_of = factor_of * one(*cut)
    return factor_of


def deal_out(own_key, own, number, rows, count, top, bound, slope):
    sequence = jax.random.permutation(own_key, count)
    heavy_load, usual = shares(count, rows * top, bound, slope, True), shares(count, rows * top, bound, slope, False)
    places = jnp.arange(count)

    def named(sizes, offset_by):
        used = int((sizes > 0).sum())
        fixed = max(1, used // 4)
        passed = fixed + (places - fixed + offset_by * (used - fixed)) % max(1, count - fixed)
        return jnp.zeros((count,), jnp.int32).at[sequence[jnp.where(places < fixed, places, passed)]].set(jnp.asarray(sizes, jnp.int32))

    sizes = jnp.where(number % 4 == 0, named(heavy_load, number // 4), named(usual, number - number // 4 - 1))
    mixed = jax.random.permutation(jax.random.fold_in(own, 3), count)
    source_of, taker = mixed[0:count // 2 * 2:2], mixed[1:count // 2 * 2:2]
    room = jnp.minimum(sizes[source_of] - 1, bound - sizes[taker]) // 2
    room = jnp.where((source_of == sequence[0]) | (taker == sequence[0]) | (sizes[taker] == 0), 0, jnp.maximum(room, 0))
    passed = jax.random.randint(jax.random.fold_in(own, 4), (count // 2,), 0, 1 << 20) % (room + 1)
    sizes = sizes.at[source_of].add(-passed).at[taker].add(passed)
    members = jnp.searchsorted(jnp.cumsum(sizes), jnp.arange(rows * top), side="right").astype(jnp.int32)
    grid = members.reshape(top, rows).T
    grid = grid[jax.random.permutation(jax.random.fold_in(own, 1), rows)]
    offset_by = jax.random.randint(jax.random.fold_in(own, 2), (rows, 1), 0, top)
    return jnp.take_along_axis(grid, (jnp.arange(top)[None, :] + offset_by) % top, axis=1)


def shares(number_of, total, limit, skew, full):
    portions = [(1 << 20) // math.isqrt(grade ** skew) + 1 for grade in range(1, number_of + 1)]
    largest = limit if full else min(limit, max(-(-total // number_of), total * portions[0] // sum(portions)))
    least = 1 if total - largest >= number_of - 1 else 0
    holding, surplus = [largest] + [least] * (number_of - 1), total - largest - least * (number_of - 1)
    while surplus > 0:
        candidates = [i for i in range(1, number_of) if holding[i] < largest] or [i for i in range(1, number_of) if holding[i] < limit]
        mass, budget = sum([portions[i] for i in candidates]), surplus
        for i in candidates:
            addition = min(limit - holding[i], max(1, budget * portions[i] // mass), surplus)
            holding[i] = holding[i] + addition
            surplus = surplus - addition
    return np.array(holding)


def noise(stream_key, shape, scale, most, pieces=(), kind=jnp.bfloat16):
    array = jax.random.normal(stream_key, shape, jnp.float32) * scale
    if len(pieces) > 0:
        array = steps_of(stream_key, shape, pieces, -0.22, 0.18) * array
    return jnp.clip(array, min=-most, max=most).astype(kind)


def gaussian_with(key, extent, scale, most, pieces, heavy, kind=jnp.bfloat16):
    entries = scale * jax.random.normal(key, extent, jnp.float32)
    if pieces:
        entries = entries * steps_of(key, extent, pieces, -0.22, 0.18)
    return jnp.clip(with_spikes(entries, jax.random.fold_in(key, 3), *heavy), -most, most).astype(kind)


def setup_inputs(seed: int = 0) -> dict:
    streams_of = jax.random.split(jax.random.key(seed), 11)
    tokens = noise(streams_of[0], (ISLANDS, STEPS, ISL_TOK, D), 1.0, 6.0, ((0, 16), (2, 16)))
    targets = noise(streams_of[1], (ISLANDS, STEPS, ISL_TOK, D), 0.5, 3.0, ((0, 16), (2, 16)))
    expert_ids_keys = jax.random.split(jax.random.fold_in(streams_of[2], 1), ISLANDS * STEPS * ISL_TOK // TOK_DEV)
    expert_ids_turns = jax.random.permutation(jax.random.fold_in(streams_of[2], 3), ISLANDS * STEPS * ISL_TOK // TOK_DEV)
    expert_ids = jax.vmap(lambda own, number: deal_out(jax.random.fold_in(streams_of[2], 2), own, number, TOK_DEV, EXPERTS, TOP, CAP, 2))(expert_ids_keys, expert_ids_turns).reshape((ISLANDS, STEPS, ISL_TOK, TOP))
    route_weight = jnp.clip(jnp.exp(math.log(1.0) - 2.9957323 * jax.random.uniform(streams_of[3], (ISLANDS, STEPS, ISL_TOK, TOP), jnp.float32) ** steps_of(streams_of[3], (ISLANDS, STEPS, ISL_TOK, TOP), ((0, 16), (2, 16)), -0.2, 0.2)), 0.05, 1.0)
    w_gate = noise(streams_of[4], (ISLANDS, EXPERTS, D, HID), 1.0, 5.0, ((0, 16), (1, 16)))
    w_up = noise(streams_of[5], (ISLANDS, EXPERTS, D, HID), 1.0, 5.0, ((0, 16), (1, 16)))
    w_down = noise(streams_of[6], (ISLANDS, EXPERTS, HID, D), 1.0, 5.0, ((0, 16), (1, 16)))
    prev_delta = gaussian_with(streams_of[7], (ISLANDS, EXPERTS, HID, D), 0.3, 2.0, ((0, 16), (1, 16)), (0, 2, 16, 2.0))
    global_params = noise(streams_of[8], (EXPERTS, HID, D), 1.0, 5.0, ((0, 16), (1, 16)), jnp.float32)
    momentum = noise(streams_of[9], (EXPERTS, HID, D), 0.3, 2.0, ((0, 16), (1, 16)), jnp.float32)
    return {"tokens": tokens, "targets": targets, "expert_ids": expert_ids, "route_weight": route_weight, "w_gate": w_gate, "w_up": w_up, "w_down": w_down, "prev_delta": prev_delta, "global_params": global_params, "momentum": momentum}


inner_rate = 4.0
outer_rate = 0.7
momentum_decay = 0.9


def slot_tables(grouped):
    devices, count = grouped.shape
    onehot = (grouped[:, :, None] == jnp.arange(EXPERTS, dtype=jnp.int32)[None, None, :]).astype(jnp.int32)
    position = jnp.sum(onehot * (jnp.cumsum(onehot, axis=1) - 1), axis=2).astype(jnp.int32)
    sender = jnp.broadcast_to(jnp.arange(devices, dtype=jnp.int32)[:, None], (devices, count))
    pair_index = jnp.arange(devices * count, dtype=jnp.int32).reshape(devices, count)
    source = jnp.zeros((EXPERTS, devices, CAP), jnp.int32).at[grouped, sender, position].set(pair_index)
    filled = jnp.zeros((EXPERTS, devices, CAP), jnp.int32).at[grouped, sender, position].set(1)
    return position, sender, source, filled


def inner_step(weights, inputs, goals, choices, scores):
    gate_weight, up_weight, down_weight = weights
    width = inputs.shape[1]
    hidden = gate_weight.shape[2]
    fanout = choices.shape[1]
    in_scale = width ** -0.5
    hid_scale = hidden ** -0.5
    grouped = choices.reshape(N_EXPERT, -1)
    position, sender, source, filled = slot_tables(grouped)
    picked_rows = jnp.take(inputs, source // fanout, axis=0)
    arrived = jnp.where(filled[..., None] > 0, picked_rows, jnp.zeros_like(picked_rows)).reshape(EXPERTS, -1, width)
    arrived_wide = arrived.astype(jnp.float32)
    pre_gate = jnp.einsum("erd,edh->erh", arrived_wide, gate_weight.astype(jnp.float32)) * in_scale
    pre_up = jnp.einsum("erd,edh->erh", arrived_wide, up_weight.astype(jnp.float32)) * in_scale
    sigmoid_gate = jax.nn.sigmoid(pre_gate)
    activated = pre_gate * sigmoid_gate
    hidden_act = (activated * pre_up).astype(jnp.bfloat16)
    produced = (jnp.einsum("erh,ehd->erd", hidden_act.astype(jnp.float32), down_weight.astype(jnp.float32)) * hid_scale).astype(jnp.bfloat16)
    returned = produced.reshape(EXPERTS, N_EXPERT, CAP, width)[grouped, sender, position]
    mixing = scores / jnp.sum(scores, axis=1, keepdims=True)
    combined = jnp.sum(mixing[:, :, None] * returned.reshape(-1, fanout, width).astype(jnp.float32), axis=1)
    residual = (combined - goals.astype(jnp.float32)).astype(jnp.bfloat16)
    pair_grad = (mixing[:, :, None] * residual[:, None, :].astype(jnp.float32)).astype(jnp.bfloat16).reshape(-1, width)
    back_rows = jnp.take(pair_grad, source.reshape(-1), axis=0).reshape(EXPERTS, N_EXPERT, CAP, width)
    out_grad = jnp.where(filled[..., None] > 0, back_rows, jnp.zeros_like(back_rows)).reshape(EXPERTS, -1, width)
    out_wide = out_grad.astype(jnp.float32)
    grad_down = jnp.einsum("erh,erd->ehd", hidden_act.astype(jnp.float32), out_wide) * hid_scale
    hidden_grad = jnp.einsum("erd,ehd->erh", out_wide, down_weight.astype(jnp.float32)) * hid_scale
    gate_grad = (hidden_grad * pre_up * sigmoid_gate * (1.0 + pre_gate * (1.0 - sigmoid_gate))).astype(jnp.bfloat16)
    up_grad = (hidden_grad * activated).astype(jnp.bfloat16)
    grad_gate = jnp.einsum("erd,erh->edh", arrived_wide, gate_grad.astype(jnp.float32)) * in_scale
    grad_up = jnp.einsum("erd,erh->edh", arrived_wide, up_grad.astype(jnp.float32)) * in_scale
    new_gate = (gate_weight.astype(jnp.float32) - inner_rate * grad_gate).astype(jnp.bfloat16)
    new_up = (up_weight.astype(jnp.float32) - inner_rate * grad_up).astype(jnp.bfloat16)
    new_down = (down_weight.astype(jnp.float32) - inner_rate * grad_down).astype(jnp.bfloat16)
    return (new_gate, new_up, new_down)


def island_round(packed):
    island_tokens, island_targets, island_ids, island_scores, gate_weight, up_weight, down_weight = packed
    weights = (gate_weight, up_weight, down_weight)
    for number in range(STEPS):
        weights = inner_step(weights, island_tokens[number], island_targets[number], island_ids[number], island_scores[number])
    return weights


def reference(tokens, targets, expert_ids, route_weight, w_gate, w_up, w_down, prev_delta, global_params, momentum):
    new_gate, new_up, new_down = lax.map(island_round, (tokens, targets, expert_ids, route_weight, w_gate, w_up, w_down))
    mean_delta = jnp.sum(prev_delta.astype(jnp.float32), axis=0) / ISLANDS
    new_momentum = momentum_decay * momentum + mean_delta
    new_global = global_params - outer_rate * (momentum_decay * new_momentum + mean_delta)
    return (new_gate, new_up, new_down, new_global, new_momentum)
```

```python
import functools

import jax
import jax.numpy as jnp
from jax import lax
from jax.experimental import pallas as pl
from jax.experimental.pallas import tpu as pltpu
from jax.sharding import Mesh, PartitionSpec as P

Z = 8
Y = 2
X = 4
A_ROWS = 64
B_ROWS = 64
LANES = 128
A_FIRST = False

inner_rate = 4.0
outer_rate = 0.7
momentum_decay = 0.9

PLUS = [(i, (i + 1) % Z) for i in range(Z)]
MINUS = [(i, (i - 1) % Z) for i in range(Z)]
SWAP = [(0, 1), (1, 0)]
ROWS = (((0,), (0,)), ((), ()))
COLS = (((1,), (1,)), ((), ()))
F32 = jnp.float32
BF16 = jnp.bfloat16
VMEM_LIMIT = 50 * 1024 * 1024
BLOCK = {512: 256, 640: 320, 768: 256, 1024: 256}


def up(v):
    return lax.ppermute(v, "z", PLUS)


def down(v):
    return lax.ppermute(v, "z", MINUS)


def swap(v):
    return lax.ppermute(v, "y", SWAP)


def total(*terms):
    return sum(t.astype(F32) for t in terms).astype(BF16)


def after(value, *earlier):
    return lax.optimization_barrier((value, *earlier))[0]


def spread_b(rows, stages=(), state=None):
    half = B_ROWS // 2
    plus, minus, groups = [rows], [rows], [(rows,)]
    for step in range(4):
        last = step == 3
        f = up(plus[-1][:half] if last else plus[-1])
        b = down(minus[-1][half:] if last else minus[-1])
        if step < len(stages):
            f, b, state = lax.optimization_barrier((f, b, stages[step](state)))
        plus.append(f)
        minus.append(b)
        groups.append((f, b))
    groups = [groups[0] + groups[1]] + groups[2:]
    mine = [jnp.concatenate(g, axis=0) for g in groups]
    theirs = [swap(m) for m in mine]
    return jnp.concatenate(mine, axis=0), jnp.concatenate(theirs, axis=0), (plus[1], minus[1]), state


def cuts(parts):
    edges = [0, 3 * B_ROWS, 5 * B_ROWS, 7 * B_ROWS, 8 * B_ROWS]
    return [parts[i:j] for i, j in zip(edges[:-1], edges[1:])]


def collect_b(mine, sent):
    n = B_ROWS
    half = n // 2
    other1, other2, other3, other4 = [swap(s) for s in sent[::-1]][::-1]
    mine1, mine2, mine3, mine4 = cuts(mine)
    f4, b4 = total(mine4[:half], other4[:half]), total(mine4[half:], other4[half:])
    r4, l4 = down(f4), up(b4)
    zeros = jnp.zeros_like(r4)
    f3 = total(mine3[:n], other3[:n], jnp.concatenate([r4, zeros], axis=0))
    b3 = total(mine3[n:], other3[n:], jnp.concatenate([zeros, l4], axis=0))
    r3, l3 = down(f3), up(b3)
    f2 = total(mine2[:n], other2[:n], r3)
    b2 = total(mine2[n:], other2[n:], l3)
    r2, l2 = down(f2), up(b2)
    f1 = total(mine1[n : 2 * n], other1[n : 2 * n], r2)
    b1 = total(mine1[2 * n :], other1[2 * n :], l2)
    r1, l1 = down(f1), up(b1)
    return mine1[:n], other1[:n], r1, l1


def mixing_columns(expert_ids, scores):
    experts = Z * Y
    mixing = scores / jnp.sum(scores, axis=1, keepdims=True)
    names = jnp.arange(experts, dtype=jnp.int32)
    dense = jnp.sum(jnp.where(expert_ids[:, :, None] == names, mixing[:, :, None], 0.0), axis=1)
    high = lax.reduce_precision(dense, exponent_bits=8, mantissa_bits=7)
    low = dense - high
    both = jnp.concatenate([high, low], axis=1).astype(BF16)
    return jnp.pad(both, ((0, 0), (0, LANES - 2 * experts)))


def forward_kernel(in_scale, hid_scale, pick, rows, w_in, w_down, out, hidden, slope_gate, slope_up):
    width, hid = w_in.shape[0], w_down.shape[0]
    mix = jnp.sum(rows[:, width:].astype(F32) * pick[...], axis=1, keepdims=True) * hid_scale
    pre = jnp.dot(rows[:, :width], w_in[...], preferred_element_type=F32) * in_scale
    pre_gate, pre_up = pre[:, :hid], pre[:, hid:]
    sig = 1.0 / (1.0 + jnp.exp(-pre_gate))
    act = pre_gate * sig
    scaled = act * mix
    hid_rows = (scaled * pre_up).astype(BF16)
    hidden[...] = hid_rows
    slope_gate[...] = pre_up * mix * sig * (1.0 + pre_gate * (1.0 - sig))
    slope_up[...] = scaled
    out[...] = jnp.dot(hid_rows, w_down[...], preferred_element_type=F32).astype(BF16)


def whole(v):
    return pl.BlockSpec(v.shape, lambda i: (0,) * v.ndim)


def cost(flops, *arrays):
    return pl.CostEstimate(
        flops=flops, bytes_accessed=sum(a.size * a.dtype.itemsize for a in arrays), transcendentals=0
    )


def forward(pick, rows, w_in, w_down):
    count, wide = rows.shape
    hid, width = w_down.shape
    block = BLOCK[count]
    outs = [
        jax.ShapeDtypeStruct((count, width), BF16),
        jax.ShapeDtypeStruct((count, hid), BF16),
        jax.ShapeDtypeStruct((count, hid), F32),
        jax.ShapeDtypeStruct((count, hid), F32),
    ]
    out, *saved = pl.pallas_call(
        functools.partial(forward_kernel, width**-0.5, hid**-0.5),
        grid=(count // block,),
        in_specs=[whole(pick), pl.BlockSpec((block, wide), lambda i: (i, 0)), whole(w_in), whole(w_down)],
        out_specs=[pl.BlockSpec((block, o.shape[1]), lambda i: (i, 0)) for o in outs],
        out_shape=outs,
        cost_estimate=cost(6 * count * width * hid, rows, w_in, w_down, *outs),
        compiler_params=pltpu.CompilerParams(vmem_limit_bytes=VMEM_LIMIT),
        name="forward",
    )(pick, rows, w_in, w_down)
    return out, (rows, *saved)


def slope_kernel(resid, w_down, slope_gate, slope_up, grads):
    hid = w_down.shape[0]
    back = lax.dot_general(resid[...], w_down[...], COLS, preferred_element_type=F32)
    grads[:, :hid] = (back * slope_gate[...]).astype(BF16)
    grads[:, hid:] = (back * slope_up[...]).astype(BF16)


def slopes(resid, w_down, saved):
    _, _, slope_gate, slope_up = saved
    count, width = resid.shape
    hid = w_down.shape[0]
    block = BLOCK[count]
    out = jax.ShapeDtypeStruct((count, 2 * hid), BF16)
    part = pl.BlockSpec((block, hid), lambda i: (i, 0))
    return pl.pallas_call(
        slope_kernel,
        grid=(count // block,),
        in_specs=[pl.BlockSpec((block, width), lambda i: (i, 0)), whole(w_down), part, part],
        out_specs=pl.BlockSpec((block, 2 * hid), lambda i: (i, 0)),
        out_shape=out,
        cost_estimate=cost(2 * count * width * hid, resid, w_down, slope_gate, slope_up, out),
        compiler_params=pltpu.CompilerParams(vmem_limit_bytes=VMEM_LIMIT),
        name="slopes",
    )(resid, w_down, slope_gate, slope_up)


def grad_kernel(pieces, started, final, in_scale, *refs):
    refs = list(refs)
    both, low = 0.0, 0.0
    for _ in range(pieces):
        rows, grads, hidden, resid = refs[:4]
        refs = refs[4:]
        both += lax.dot_general(rows[...], grads[...], ROWS, preferred_element_type=F32)
        low += lax.dot_general(hidden[...], resid[...], ROWS, preferred_element_type=F32)
    if started:
        both += refs[0][...]
        low += refs[1][...]
        refs = refs[2:]
    if not final:
        refs[0][...] = both
        refs[1][...] = low
        return
    w_gate, w_up, w_down, new_gate, new_up, new_down = refs
    hid = w_gate.shape[1]
    step = inner_rate * in_scale
    new_gate[...] = (w_gate[...].astype(F32) - step * both[:, :hid]).astype(BF16)
    new_up[...] = (w_up[...].astype(F32) - step * both[:, hid:]).astype(BF16)
    new_down[...] = (w_down[...].astype(F32) - inner_rate * low).astype(BF16)


def gradients(pieces, started=None, weights=None, tile=256):
    hid = pieces[0][2].shape[1]
    width = pieces[0][3].shape[1]
    by_row = lambda n: pl.BlockSpec((tile, n), lambda i: (i, 0))
    by_col = lambda n: pl.BlockSpec((n, tile), lambda i: (0, i))
    args, specs = [], []
    flops = 0
    for rows, grads, hidden, resid in pieces:
        n = rows.shape[0]
        args += [rows, grads, hidden, resid]
        specs += [by_col(n), whole(grads), whole(hidden), by_col(n)]
        flops += 6 * n * hid * width
    if started is not None:
        args += list(started)
        specs += [by_row(2 * hid), by_col(hid)]
    if weights is None:
        outs = [jax.ShapeDtypeStruct((width, 2 * hid), F32), jax.ShapeDtypeStruct((hid, width), F32)]
        out_specs = [by_row(2 * hid), by_col(hid)]
    else:
        args += list(weights)
        out_specs = [by_row(hid), by_row(hid), by_col(hid)]
        specs += out_specs
        outs = [jax.ShapeDtypeStruct(w.shape, BF16) for w in weights]
    return pl.pallas_call(
        functools.partial(grad_kernel, len(pieces), started is not None, weights is not None, width**-0.5),
        grid=(width // tile,),
        in_specs=specs,
        out_specs=out_specs,
        out_shape=outs,
        cost_estimate=cost(flops, *args, *outs),
        compiler_params=pltpu.CompilerParams(vmem_limit_bytes=VMEM_LIMIT),
        name="gradients" if weights is None else "update",
    )(*args)


def halve(parts, axis, pairs, dim, bit):
    low, high = lax.index_in_dim(parts, 0, dim, False), lax.index_in_dim(parts, 1, dim, False)
    first = bit == 0
    sent = jnp.where(first, high, low)
    kept = jnp.where(first, low, high)
    return total(kept, lax.ppermute(sent, axis, pairs))


def outer_stages():
    x = lax.axis_index("x")
    return [
        lambda d: halve(d, "core", SWAP, 3, lax.axis_index("core")),
        lambda d: halve(d, "x", [(i, i ^ 1) for i in range(X)], 1, x % 2),
        lambda d: halve(d, "x", [(i, i ^ 2) for i in range(X)], 0, x // 2),
        lambda d: halve(d, "yh", SWAP, 0, lax.axis_index("yh")),
    ]


def outer_update(share, global_params, momentum, islands):
    mean_delta = share.astype(F32) / islands
    new_momentum = momentum_decay * momentum + mean_delta
    new_global = global_params - outer_rate * (momentum_decay * new_momentum + mean_delta)
    return new_global, new_momentum


def shards(tokens, targets, expert_ids, route_weight, w_gate, w_up, w_down, prev_delta, global_params, momentum):
    tokens, targets = tokens[0, 0], targets[0, 0]
    weights = w_gate, w_up, w_down = w_gate[0, 0], w_up[0, 0], w_down[0, 0]
    expert = lax.axis_index("z") * Y + lax.axis_index("y")
    lane = jnp.arange(LANES, dtype=jnp.int32)[None, :]
    pick = ((lane == expert) | (lane == Z * Y + expert)).astype(F32)
    marked = jnp.concatenate([tokens, mixing_columns(expert_ids[0, 0], route_weight[0, 0])], axis=1)

    goal_own, goal_b = targets[:A_ROWS], targets[A_ROWS:]
    goal_pair = jnp.concatenate([goal_own, swap(goal_own)], axis=0).astype(F32)
    w_in = jnp.concatenate([w_gate, w_up], axis=1)
    parts = prev_delta[0, 0].reshape(2, 2, 2, 2, -1, w_gate.shape[0])

    pair = jnp.concatenate([marked[:A_ROWS], swap(marked[:A_ROWS])], axis=0)
    rows_a = lax.all_gather(pair, "z", axis=0, tiled=True)
    rows_b, rows_c, _, share = spread_b(marked[A_ROWS:], outer_stages(), parts)
    out_b, saved_b = forward(pick, rows_b, w_in, w_down)
    if A_FIRST:
        out_a, saved_a = forward(pick, after(rows_a, out_b), w_in, w_down)
        out_c, saved_c = forward(pick, after(rows_c, out_a), w_in, w_down)
        sent_c = cuts(out_c)
    else:
        out_c, saved_c = forward(pick, after(rows_c, out_b), w_in, w_down)
        sent_c = cuts(out_c)
        out_a, saved_a = forward(pick, after(rows_a, *sent_c), w_in, w_down)
    pair_a = lax.psum_scatter(out_a, "z", scatter_dimension=0, tiled=True)
    resid_b = (sum(t.astype(F32) for t in collect_b(out_b, sent_c)) - goal_b.astype(F32)).astype(BF16)
    pair_a = after(pair_a, resid_b)
    turned = swap(pair_a)
    back_b, back_c, first, _ = spread_b(resid_b)
    turned = after(turned, *first)
    turned = jnp.concatenate([turned[A_ROWS:], turned[:A_ROWS]], axis=0)
    resid_a = (pair_a.astype(F32) + turned.astype(F32) - goal_pair).astype(BF16)
    back_a = lax.all_gather(resid_a, "z", axis=0, tiled=True)
    grads_b = slopes(back_b, w_down, saved_b)
    grads_c = slopes(back_c, w_down, saved_c)
    grads_a = slopes(after(back_a, grads_b, grads_c), w_down, saved_a)
    pieces = [(s[0], g, s[1], r) for s, g, r in ((saved_b, grads_b, back_b), (saved_c, grads_c, back_c), (saved_a, grads_a, back_a))]
    new = gradients(pieces, None, weights)
    islands = X * Y * 2
    new_global, new_momentum = outer_update(share, global_params[0], momentum[0], islands)
    return (*[w[None, None] for w in new], new_global[None], new_momentum[None])


def solution(mesh):
    fine = Mesh(mesh.devices.reshape(X, 2, 2, Z, Y), ("x", "yh", "core", "z", "y"))
    island = ("x", "yh", "core")
    expert = ("z", "y")
    tok = P(island, None, expert, None)
    wgt = P(island, expert, None, None)
    out = P(expert, island, None)
    return jax.shard_map(
        shards,
        mesh=fine,
        in_specs=(tok, tok, tok, tok, wgt, wgt, wgt, wgt, out, out),
        out_specs=(wgt, wgt, wgt, out, out),
        check_vma=False,
    )
```

```python
import functools

import jax
import jax.numpy as jnp
from jax import lax
from jax.experimental import pallas as pl
from jax.experimental.pallas import tpu as pltpu
from jax.sharding import Mesh, PartitionSpec as P

Z = 8
Y = 2
X = 4
A_ROWS = 64
B_ROWS = 64
LANES = 128

inner_rate = 4.0
outer_rate = 0.7
momentum_decay = 0.9

PLUS = [(i, (i + 1) % Z) for i in range(Z)]
MINUS = [(i, (i - 1) % Z) for i in range(Z)]
SWAP = [(0, 1), (1, 0)]
ROWS = (((0,), (0,)), ((), ()))
COLS = (((1,), (1,)), ((), ()))
F32 = jnp.float32
BF16 = jnp.bfloat16
MIB = 1024 * 1024
FORWARD_VMEM = 60 * MIB
SLOPES_VMEM = 50 * MIB
UPDATE_VMEM = 50 * MIB
BLOCK = {512: 256, 640: 320, 768: 256, 1024: 256}


def up(v):
    return lax.ppermute(v, "z", PLUS)


def down(v):
    return lax.ppermute(v, "z", MINUS)


def swap(v):
    return lax.ppermute(v, "y", SWAP)


def total(*terms):
    return sum(t.astype(F32) for t in terms).astype(BF16)


def after(value, *earlier):
    return lax.optimization_barrier((value, *earlier))[0]


def spread_b(rows, stages=(), state=None):
    half = B_ROWS // 2
    plus, minus, groups = [rows], [rows], [(rows,)]
    for step in range(4):
        last = step == 3
        f = up(plus[-1][:half] if last else plus[-1])
        b = down(minus[-1][half:] if last else minus[-1])
        if step < len(stages):
            f, b, state = lax.optimization_barrier((f, b, stages[step](state)))
        plus.append(f)
        minus.append(b)
        groups.append((f, b))
    groups = [groups[0] + groups[1]] + groups[2:]
    mine = [jnp.concatenate(g, axis=0) for g in groups]
    theirs = [swap(m) for m in mine]
    return jnp.concatenate(mine, axis=0), jnp.concatenate(theirs, axis=0), (plus[1], minus[1]), state


def cuts(parts):
    edges = [0, 3 * B_ROWS, 5 * B_ROWS, 7 * B_ROWS, 8 * B_ROWS]
    return [parts[i:j] for i, j in zip(edges[:-1], edges[1:])]


def collect_b(mine, sent):
    n = B_ROWS
    half = n // 2
    other1, other2, other3, other4 = [swap(s) for s in sent[::-1]][::-1]
    mine1, mine2, mine3, mine4 = cuts(mine)
    f4, b4 = total(mine4[:half], other4[:half]), total(mine4[half:], other4[half:])
    r4, l4 = down(f4), up(b4)
    zeros = jnp.zeros_like(r4)
    f3 = total(mine3[:n], other3[:n], jnp.concatenate([r4, zeros], axis=0))
    b3 = total(mine3[n:], other3[n:], jnp.concatenate([zeros, l4], axis=0))
    r3, l3 = down(f3), up(b3)
    f2 = total(mine2[:n], other2[:n], r3)
    b2 = total(mine2[n:], other2[n:], l3)
    r2, l2 = down(f2), up(b2)
    f1 = total(mine1[n : 2 * n], other1[n : 2 * n], r2)
    b1 = total(mine1[2 * n :], other1[2 * n :], l2)
    r1, l1 = down(f1), up(b1)
    return mine1[:n], other1[:n], r1, l1


def mixing_columns(expert_ids, scores):
    experts = Z * Y
    mixing = scores / jnp.sum(scores, axis=1, keepdims=True)
    names = jnp.arange(experts, dtype=jnp.int32)
    dense = jnp.sum(jnp.where(expert_ids[:, :, None] == names, mixing[:, :, None], 0.0), axis=1)
    high = lax.reduce_precision(dense, exponent_bits=8, mantissa_bits=7)
    low = dense - high
    both = jnp.concatenate([high, low], axis=1).astype(BF16)
    return jnp.pad(both, ((0, 0), (0, LANES - 2 * experts)))


def forward_kernel(in_scale, hid_scale, pick, rows, w_gate, w_up, w_down, out, hidden, slope_gate, slope_up):
    width = w_gate.shape[0]
    mix = jnp.sum(rows[:, width:].astype(F32) * pick[...], axis=1, keepdims=True) * hid_scale
    x = rows[:, :width]
    pre_gate = jnp.dot(x, w_gate[...], preferred_element_type=F32) * in_scale
    pre_up = jnp.dot(x, w_up[...], preferred_element_type=F32) * in_scale
    sig = 1.0 / (1.0 + jnp.exp(-pre_gate))
    act = pre_gate * sig
    scaled = act * mix
    hid_rows = (scaled * pre_up).astype(BF16)
    hidden[...] = hid_rows
    slope_gate[...] = pre_up * mix * sig * (1.0 + pre_gate * (1.0 - sig))
    slope_up[...] = scaled
    out[...] = jnp.dot(hid_rows, w_down[...], preferred_element_type=F32).astype(BF16)


def whole(v):
    return pl.BlockSpec(v.shape, lambda i: (0,) * v.ndim)


def cost(flops, *arrays):
    return pl.CostEstimate(
        flops=flops, bytes_accessed=sum(a.size * a.dtype.itemsize for a in arrays), transcendentals=0
    )


def forward(pick, rows, w_gate, w_up, w_down):
    count, wide = rows.shape
    hid, width = w_down.shape
    block = BLOCK[count]
    outs = [
        jax.ShapeDtypeStruct((count, width), BF16),
        jax.ShapeDtypeStruct((count, hid), BF16),
        jax.ShapeDtypeStruct((count, hid), F32),
        jax.ShapeDtypeStruct((count, hid), F32),
    ]
    args = (pick, rows, w_gate, w_up, w_down)
    out, *saved = pl.pallas_call(
        functools.partial(forward_kernel, width**-0.5, hid**-0.5),
        grid=(count // block,),
        in_specs=[pl.BlockSpec((block, wide), lambda i: (i, 0)) if v is rows else whole(v) for v in args],
        out_specs=[pl.BlockSpec((block, o.shape[1]), lambda i: (i, 0)) for o in outs],
        out_shape=outs,
        cost_estimate=cost(6 * count * width * hid, *args, *outs),
        compiler_params=pltpu.CompilerParams(vmem_limit_bytes=FORWARD_VMEM),
        name="forward",
    )(*args)
    return out, (rows, *saved)


def slope_kernel(resid, w_down, slope_gate, slope_up, grads):
    hid = w_down.shape[0]
    back = lax.dot_general(resid[...], w_down[...], COLS, preferred_element_type=F32)
    grads[:, :hid] = (back * slope_gate[...]).astype(BF16)
    grads[:, hid:] = (back * slope_up[...]).astype(BF16)


def slopes(resid, w_down, saved):
    _, _, slope_gate, slope_up = saved
    count, width = resid.shape
    hid = w_down.shape[0]
    block = BLOCK[count]
    out = jax.ShapeDtypeStruct((count, 2 * hid), BF16)
    part = pl.BlockSpec((block, hid), lambda i: (i, 0))
    return pl.pallas_call(
        slope_kernel,
        grid=(count // block,),
        in_specs=[pl.BlockSpec((block, width), lambda i: (i, 0)), whole(w_down), part, part],
        out_specs=pl.BlockSpec((block, 2 * hid), lambda i: (i, 0)),
        out_shape=out,
        cost_estimate=cost(2 * count * width * hid, resid, w_down, slope_gate, slope_up, out),
        compiler_params=pltpu.CompilerParams(vmem_limit_bytes=SLOPES_VMEM),
        name="slopes",
    )(resid, w_down, slope_gate, slope_up)


def grad_kernel(pieces, started, final, in_scale, *refs):
    refs = list(refs)
    both, low = 0.0, 0.0
    for _ in range(pieces):
        rows, grads, hidden, resid = refs[:4]
        refs = refs[4:]
        both += lax.dot_general(rows[...], grads[...], ROWS, preferred_element_type=F32)
        low += lax.dot_general(hidden[...], resid[...], ROWS, preferred_element_type=F32)
    if started:
        both += refs[0][...]
        low += refs[1][...]
        refs = refs[2:]
    if not final:
        refs[0][...] = both
        refs[1][...] = low
        return
    w_gate, w_up, w_down, new_gate, new_up, new_down = refs
    hid = w_gate.shape[1]
    step = inner_rate * in_scale
    new_gate[...] = (w_gate[...].astype(F32) - step * both[:, :hid]).astype(BF16)
    new_up[...] = (w_up[...].astype(F32) - step * both[:, hid:]).astype(BF16)
    new_down[...] = (w_down[...].astype(F32) - inner_rate * low).astype(BF16)


def gradients(pieces, started=None, weights=None, tile=512):
    hid = pieces[0][2].shape[1]
    width = pieces[0][3].shape[1]
    by_row = lambda n: pl.BlockSpec((tile, n), lambda i: (i, 0))
    by_col = lambda n: pl.BlockSpec((n, tile), lambda i: (0, i))
    args, specs = [], []
    flops = 0
    for rows, grads, hidden, resid in pieces:
        n = rows.shape[0]
        args += [rows, grads, hidden, resid]
        specs += [by_col(n), whole(grads), whole(hidden), by_col(n)]
        flops += 6 * n * hid * width
    if started is not None:
        args += list(started)
        specs += [by_row(2 * hid), by_col(hid)]
    if weights is None:
        outs = [jax.ShapeDtypeStruct((width, 2 * hid), F32), jax.ShapeDtypeStruct((hid, width), F32)]
        out_specs = [by_row(2 * hid), by_col(hid)]
    else:
        args += list(weights)
        out_specs = [by_row(hid), by_row(hid), by_col(hid)]
        specs += out_specs
        outs = [jax.ShapeDtypeStruct(w.shape, BF16) for w in weights]
    return pl.pallas_call(
        functools.partial(grad_kernel, len(pieces), started is not None, weights is not None, width**-0.5),
        grid=(width // tile,),
        in_specs=specs,
        out_specs=out_specs,
        out_shape=outs,
        cost_estimate=cost(flops, *args, *outs),
        compiler_params=pltpu.CompilerParams(vmem_limit_bytes=UPDATE_VMEM),
        name="gradients" if weights is None else "update",
    )(*args)


def halve(parts, axis, pairs, dim, bit):
    low, high = lax.index_in_dim(parts, 0, dim, False), lax.index_in_dim(parts, 1, dim, False)
    first = bit == 0
    sent = jnp.where(first, high, low)
    kept = jnp.where(first, low, high)
    return total(kept, lax.ppermute(sent, axis, pairs))


def outer_stages():
    x = lax.axis_index("x")
    return [
        lambda d: halve(d, "core", SWAP, 3, lax.axis_index("core")),
        lambda d: halve(d, "x", [(i, i ^ 1) for i in range(X)], 1, x % 2),
        lambda d: halve(d, "x", [(i, i ^ 2) for i in range(X)], 0, x // 2),
        lambda d: halve(d, "yh", SWAP, 0, lax.axis_index("yh")),
    ]


def outer_update(share, global_params, momentum, islands):
    mean_delta = share.astype(F32) / islands
    new_momentum = momentum_decay * momentum + mean_delta
    new_global = global_params - outer_rate * (momentum_decay * new_momentum + mean_delta)
    return new_global, new_momentum


def shards(tokens, targets, expert_ids, route_weight, w_gate, w_up, w_down, prev_delta, global_params, momentum):
    tokens, targets = tokens[0, 0], targets[0, 0]
    weights = w_gate, w_up, w_down = w_gate[0, 0], w_up[0, 0], w_down[0, 0]
    expert = lax.axis_index("z") * Y + lax.axis_index("y")
    lane = jnp.arange(LANES, dtype=jnp.int32)[None, :]
    pick = ((lane == expert) | (lane == Z * Y + expert)).astype(F32)
    marked = jnp.concatenate([tokens, mixing_columns(expert_ids[0, 0], route_weight[0, 0])], axis=1)

    goal_own, goal_b = targets[:A_ROWS], targets[A_ROWS:]
    parts = prev_delta[0, 0].reshape(2, 2, 2, 2, -1, w_gate.shape[0])

    pair = jnp.concatenate([marked[:A_ROWS], swap(marked[:A_ROWS])], axis=0)
    rows_a = lax.all_gather(pair, "z", axis=0, tiled=True)
    outer = outer_stages()
    early = [
        lambda s: (jnp.concatenate([s[0], swap(s[0])], axis=0), s[1]),
        lambda s: (s[0], outer[0](s[1])),
        lambda s: (s[0], outer[1](s[1])),
        lambda s: (s[0], outer[2](s[1])),
    ]
    rows_b, rows_c, _, (goal_pair, share) = spread_b(marked[A_ROWS:], early, (goal_own, after(parts, pair)))
    out_b, saved_b = forward(pick, rows_b, *weights)
    out_a, saved_a = forward(pick, after(rows_a, rows_c, out_b), *weights)
    out_c, saved_c = forward(pick, after(rows_c, out_a), *weights)
    share = outer[3](after(share, out_c))
    summed = collect_b(out_b, cuts(out_c))
    pair_a = lax.psum_scatter(out_a, "z", scatter_dimension=0, tiled=True)
    resid_b = (sum(t.astype(F32) for t in summed) - goal_b.astype(F32)).astype(BF16)
    pair_a = after(pair_a, resid_b)
    turned = swap(pair_a)
    back_b, back_c, first, _ = spread_b(resid_b)
    turned = after(turned, *first)
    turned = jnp.concatenate([turned[A_ROWS:], turned[:A_ROWS]], axis=0)
    resid_a = (pair_a.astype(F32) + turned.astype(F32) - goal_pair.astype(F32)).astype(BF16)
    back_a = lax.all_gather(resid_a, "z", axis=0, tiled=True)
    grads_b = slopes(back_b, w_down, saved_b)
    grads_c = slopes(back_c, w_down, saved_c)
    grads_a = slopes(after(back_a, grads_b, grads_c), w_down, saved_a)
    pieces = [(s[0], g, s[1], r) for s, g, r in ((saved_b, grads_b, back_b), (saved_c, grads_c, back_c), (saved_a, grads_a, back_a))]
    new = gradients(pieces, None, weights)
    islands = X * Y * 2
    new_global, new_momentum = outer_update(share, global_params[0], momentum[0], islands)
    return (*[w[None, None] for w in new], new_global[None], new_momentum[None])


def solution(mesh):
    fine = Mesh(mesh.devices.reshape(X, 2, 2, Z, Y), ("x", "yh", "core", "z", "y"))
    island = ("x", "yh", "core")
    expert = ("z", "y")
    tok = P(island, None, expert, None)
    wgt = P(island, expert, None, None)
    out = P(expert, island, None)
    return jax.shard_map(
        shards,
        mesh=fine,
        in_specs=(tok, tok, tok, tok, wgt, wgt, wgt, wgt, out, out),
        out_specs=(wgt, wgt, wgt, out, out),
        check_vma=False,
    )
```

```python
import functools

import jax
import jax.numpy as jnp
from jax import lax
from jax.experimental import pallas as pl
from jax.experimental.pallas import tpu as pltpu
from jax.sharding import Mesh, PartitionSpec as P

Z = 8
Y = 2
X = 4
A_ROWS = 64
B_ROWS = 64
LANES = 128

inner_rate = 4.0
outer_rate = 0.7
momentum_decay = 0.9

PLUS = [(i, (i + 1) % Z) for i in range(Z)]
MINUS = [(i, (i - 1) % Z) for i in range(Z)]
SWAP = [(0, 1), (1, 0)]
ROWS = (((0,), (0,)), ((), ()))
COLS = (((1,), (1,)), ((), ()))
F32 = jnp.float32
BF16 = jnp.bfloat16
MIB = 1024 * 1024
FORWARD_VMEM = 60 * MIB
SLOPES_VMEM = 50 * MIB
UPDATE_VMEM = 50 * MIB
BLOCK = {512: 256, 640: 320, 768: 256, 1024: 256}


def up(v):
    return lax.ppermute(v, "z", PLUS)


def down(v):
    return lax.ppermute(v, "z", MINUS)


def swap(v):
    return lax.ppermute(v, "y", SWAP)


def total(*terms):
    return sum(t.astype(F32) for t in terms).astype(BF16)


def after(value, *earlier):
    return lax.optimization_barrier((value, *earlier))[0]


def spread_b(rows, stages=(), state=None):
    half = B_ROWS // 2
    plus, minus, groups = [rows], [rows], [(rows,)]
    for step in range(4):
        last = step == 3
        f = up(plus[-1][:half] if last else plus[-1])
        b = down(minus[-1][half:] if last else minus[-1])
        if step < len(stages):
            f, b, state = lax.optimization_barrier((f, b, stages[step](state)))
        plus.append(f)
        minus.append(b)
        groups.append((f, b))
    groups = [groups[0] + groups[1]] + groups[2:]
    mine = [jnp.concatenate(g, axis=0) for g in groups]
    theirs = [swap(m) for m in mine]
    return jnp.concatenate(mine, axis=0), jnp.concatenate(theirs, axis=0), (plus[1], minus[1]), state


def cuts(parts):
    edges = [0, 3 * B_ROWS, 5 * B_ROWS, 7 * B_ROWS, 8 * B_ROWS]
    return [parts[i:j] for i, j in zip(edges[:-1], edges[1:])]


def collect_b(mine, sent):
    n = B_ROWS
    half = n // 2
    other1, other2, other3, other4 = [swap(s) for s in sent[::-1]][::-1]
    mine1, mine2, mine3, mine4 = cuts(mine)
    f4, b4 = total(mine4[:half], other4[:half]), total(mine4[half:], other4[half:])
    r4, l4 = down(f4), up(b4)
    zeros = jnp.zeros_like(r4)
    f3 = total(mine3[:n], other3[:n], jnp.concatenate([r4, zeros], axis=0))
    b3 = total(mine3[n:], other3[n:], jnp.concatenate([zeros, l4], axis=0))
    r3, l3 = down(f3), up(b3)
    f2 = total(mine2[:n], other2[:n], r3)
    b2 = total(mine2[n:], other2[n:], l3)
    r2, l2 = down(f2), up(b2)
    f1 = total(mine1[n : 2 * n], other1[n : 2 * n], r2)
    b1 = total(mine1[2 * n :], other1[2 * n :], l2)
    r1, l1 = down(f1), up(b1)
    return mine1[:n], other1[:n], r1, l1


def mixing_columns(expert_ids, scores):
    experts = Z * Y
    mixing = scores / jnp.sum(scores, axis=1, keepdims=True)
    names = jnp.arange(experts, dtype=jnp.int32)
    dense = jnp.sum(jnp.where(expert_ids[:, :, None] == names, mixing[:, :, None], 0.0), axis=1)
    high = lax.reduce_precision(dense, exponent_bits=8, mantissa_bits=7)
    low = dense - high
    both = jnp.concatenate([high, low], axis=1).astype(BF16)
    return jnp.pad(both, ((0, 0), (0, LANES - 2 * experts)))


def forward_kernel(in_scale, hid_scale, pick, rows, w_gate, w_up, w_down, out, hidden, slope_gate, slope_up):
    width = w_gate.shape[0]
    mix = jnp.sum(rows[:, width:].astype(F32) * pick[...], axis=1, keepdims=True) * hid_scale
    x = rows[:, :width]
    pre_gate = jnp.dot(x, w_gate[...], preferred_element_type=F32) * in_scale
    pre_up = jnp.dot(x, w_up[...], preferred_element_type=F32) * in_scale
    sig = 1.0 / (1.0 + jnp.exp(-pre_gate))
    act = pre_gate * sig
    scaled = act * mix
    hid_rows = (scaled * pre_up).astype(BF16)
    hidden[...] = hid_rows
    slope_gate[...] = pre_up * mix * sig * (1.0 + pre_gate * (1.0 - sig))
    slope_up[...] = scaled
    out[...] = jnp.dot(hid_rows, w_down[...], preferred_element_type=F32).astype(BF16)


def whole(v):
    return pl.BlockSpec(v.shape, lambda i: (0,) * v.ndim)


def cost(flops, *arrays):
    return pl.CostEstimate(
        flops=flops, bytes_accessed=sum(a.size * a.dtype.itemsize for a in arrays), transcendentals=0
    )


def forward(pick, rows, w_gate, w_up, w_down):
    count, wide = rows.shape
    hid, width = w_down.shape
    block = BLOCK[count]
    outs = [
        jax.ShapeDtypeStruct((count, width), BF16),
        jax.ShapeDtypeStruct((count, hid), BF16),
        jax.ShapeDtypeStruct((count, hid), F32),
        jax.ShapeDtypeStruct((count, hid), F32),
    ]
    args = (pick, rows, w_gate, w_up, w_down)
    out, *saved = pl.pallas_call(
        functools.partial(forward_kernel, width**-0.5, hid**-0.5),
        grid=(count // block,),
        in_specs=[pl.BlockSpec((block, wide), lambda i: (i, 0)) if v is rows else whole(v) for v in args],
        out_specs=[pl.BlockSpec((block, o.shape[1]), lambda i: (i, 0)) for o in outs],
        out_shape=outs,
        cost_estimate=cost(6 * count * width * hid, *args, *outs),
        compiler_params=pltpu.CompilerParams(vmem_limit_bytes=FORWARD_VMEM),
        name="forward",
    )(*args)
    return out, (rows, *saved)


def slope_kernel(resid, w_down, slope_gate, slope_up, grads):
    hid = w_down.shape[0]
    back = lax.dot_general(resid[...], w_down[...], COLS, preferred_element_type=F32)
    grads[:, :hid] = (back * slope_gate[...]).astype(BF16)
    grads[:, hid:] = (back * slope_up[...]).astype(BF16)


def slopes(resid, w_down, saved):
    _, _, slope_gate, slope_up = saved
    count, width = resid.shape
    hid = w_down.shape[0]
    block = count // 2
    out = jax.ShapeDtypeStruct((count, 2 * hid), BF16)
    part = pl.BlockSpec((block, hid), lambda i: (i, 0))
    return pl.pallas_call(
        slope_kernel,
        grid=(count // block,),
        in_specs=[pl.BlockSpec((block, width), lambda i: (i, 0)), whole(w_down), part, part],
        out_specs=pl.BlockSpec((block, 2 * hid), lambda i: (i, 0)),
        out_shape=out,
        cost_estimate=cost(2 * count * width * hid, resid, w_down, slope_gate, slope_up, out),
        compiler_params=pltpu.CompilerParams(vmem_limit_bytes=SLOPES_VMEM),
        name="slopes",
    )(resid, w_down, slope_gate, slope_up)


def grad_kernel(pieces, started, final, in_scale, *refs):
    refs = list(refs)
    both, low = 0.0, 0.0
    for _ in range(pieces):
        rows, grads, hidden, resid = refs[:4]
        refs = refs[4:]
        both += lax.dot_general(rows[...], grads[...], ROWS, preferred_element_type=F32)
        low += lax.dot_general(hidden[...], resid[...], ROWS, preferred_element_type=F32)
    if started:
        both += refs[0][...]
        low += refs[1][...]
        refs = refs[2:]
    if not final:
        refs[0][...] = both
        refs[1][...] = low
        return
    w_gate, w_up, w_down, new_gate, new_up, new_down = refs
    hid = w_gate.shape[1]
    step = inner_rate * in_scale
    new_gate[...] = (w_gate[...].astype(F32) - step * both[:, :hid]).astype(BF16)
    new_up[...] = (w_up[...].astype(F32) - step * both[:, hid:]).astype(BF16)
    new_down[...] = (w_down[...].astype(F32) - inner_rate * low).astype(BF16)


def gradients(pieces, started=None, weights=None, tile=512):
    hid = pieces[0][2].shape[1]
    width = pieces[0][3].shape[1]
    by_row = lambda n: pl.BlockSpec((tile, n), lambda i: (i, 0))
    by_col = lambda n: pl.BlockSpec((n, tile), lambda i: (0, i))
    args, specs = [], []
    flops = 0
    for rows, grads, hidden, resid in pieces:
        n = rows.shape[0]
        args += [rows, grads, hidden, resid]
        specs += [by_col(n), whole(grads), whole(hidden), by_col(n)]
        flops += 6 * n * hid * width
    if started is not None:
        args += list(started)
        specs += [by_row(2 * hid), by_col(hid)]
    if weights is None:
        outs = [jax.ShapeDtypeStruct((width, 2 * hid), F32), jax.ShapeDtypeStruct((hid, width), F32)]
        out_specs = [by_row(2 * hid), by_col(hid)]
    else:
        args += list(weights)
        out_specs = [by_row(hid), by_row(hid), by_col(hid)]
        specs += out_specs
        outs = [jax.ShapeDtypeStruct(w.shape, BF16) for w in weights]
    return pl.pallas_call(
        functools.partial(grad_kernel, len(pieces), started is not None, weights is not None, width**-0.5),
        grid=(width // tile,),
        in_specs=specs,
        out_specs=out_specs,
        out_shape=outs,
        cost_estimate=cost(flops, *args, *outs),
        compiler_params=pltpu.CompilerParams(vmem_limit_bytes=UPDATE_VMEM),
        name="gradients" if weights is None else "update",
    )(*args)


def halve(parts, axis, pairs, dim, bit):
    low, high = lax.index_in_dim(parts, 0, dim, False), lax.index_in_dim(parts, 1, dim, False)
    first = bit == 0
    sent = jnp.where(first, high, low)
    kept = jnp.where(first, low, high)
    return total(kept, lax.ppermute(sent, axis, pairs))


def outer_stages():
    x = lax.axis_index("x")
    return [
        lambda d: halve(d, "core", SWAP, 3, lax.axis_index("core")),
        lambda d: halve(d, "x", [(i, i ^ 1) for i in range(X)], 1, x % 2),
        lambda d: halve(d, "x", [(i, i ^ 2) for i in range(X)], 0, x // 2),
        lambda d: halve(d, "yh", SWAP, 0, lax.axis_index("yh")),
    ]


def outer_update(share, global_params, momentum, islands):
    mean_delta = share.astype(F32) / islands
    new_momentum = momentum_decay * momentum + mean_delta
    new_global = global_params - outer_rate * (momentum_decay * new_momentum + mean_delta)
    return new_global, new_momentum


def shards(tokens, targets, expert_ids, route_weight, w_gate, w_up, w_down, prev_delta, global_params, momentum):
    tokens, targets = tokens[0, 0], targets[0, 0]
    weights = w_gate, w_up, w_down = w_gate[0, 0], w_up[0, 0], w_down[0, 0]
    expert = lax.axis_index("z") * Y + lax.axis_index("y")
    lane = jnp.arange(LANES, dtype=jnp.int32)[None, :]
    pick = ((lane == expert) | (lane == Z * Y + expert)).astype(F32)
    marked = jnp.concatenate([tokens, mixing_columns(expert_ids[0, 0], route_weight[0, 0])], axis=1)

    goal_own, goal_b = targets[:A_ROWS], targets[A_ROWS:]
    parts = prev_delta[0, 0].reshape(2, 2, 2, 2, -1, w_gate.shape[0])

    pair = jnp.concatenate([marked[:A_ROWS], swap(marked[:A_ROWS])], axis=0)
    rows_a = lax.all_gather(pair, "z", axis=0, tiled=True)
    outer = outer_stages()
    early = [
        lambda s: (jnp.concatenate([s[0], swap(s[0])], axis=0), s[1]),
        lambda s: (s[0], outer[0](s[1])),
        lambda s: (s[0], outer[1](s[1])),
        lambda s: (s[0], outer[2](s[1])),
    ]
    rows_b, rows_c, _, (goal_pair, share) = spread_b(marked[A_ROWS:], early, (goal_own, after(parts, pair)))
    out_b, saved_b = forward(pick, rows_b, *weights)
    share = outer[3](after(share, out_b))
    out_a, saved_a = forward(pick, after(rows_a, rows_c, out_b, share), *weights)
    out_c, saved_c = forward(pick, after(rows_c, out_a), *weights)
    summed = collect_b(out_b, cuts(out_c))
    pair_a = lax.psum_scatter(out_a, "z", scatter_dimension=0, tiled=True)
    resid_b = (sum(t.astype(F32) for t in summed) - goal_b.astype(F32)).astype(BF16)
    pair_a = after(pair_a, resid_b)
    turned = swap(pair_a)
    back_b, back_c, first, _ = spread_b(resid_b)
    turned = after(turned, *first)
    turned = jnp.concatenate([turned[A_ROWS:], turned[:A_ROWS]], axis=0)
    resid_a = (pair_a.astype(F32) + turned.astype(F32) - goal_pair.astype(F32)).astype(BF16)
    back_a = lax.all_gather(resid_a, "z", axis=0, tiled=True)
    grads_b = slopes(back_b, w_down, saved_b)
    grads_c = slopes(back_c, w_down, saved_c)
    grads_a = slopes(after(back_a, grads_b, grads_c), w_down, saved_a)
    pieces = [(s[0], g, s[1], r) for s, g, r in ((saved_b, grads_b, back_b), (saved_c, grads_c, back_c), (saved_a, grads_a, back_a))]
    new = gradients(pieces, None, weights)
    islands = X * Y * 2
    new_global, new_momentum = outer_update(share, global_params[0], momentum[0], islands)
    return (*[w[None, None] for w in new], new_global[None], new_momentum[None])


def solution(mesh):
    fine = Mesh(mesh.devices.reshape(X, 2, 2, Z, Y), ("x", "yh", "core", "z", "y"))
    island = ("x", "yh", "core")
    expert = ("z", "y")
    tok = P(island, None, expert, None)
    wgt = P(island, expert, None, None)
    out = P(expert, island, None)
    return jax.shard_map(
        shards,
        mesh=fine,
        in_specs=(tok, tok, tok, tok, wgt, wgt, wgt, wgt, out, out),
        out_specs=(wgt, wgt, wgt, out, out),
        check_vma=False,
    )
```
